32 devices in a mesh: ctx: 8 (over y, x, core), head: 4 (over z).
Axes of the slice: x: 2, y: 2, z: 4, core: 2. Of those that a mesh axis runs over, the one named last changes fastest.
Arguments:
- mixer_in: bfloat16 [1536, 16384], P('ctx', 'head'), may hold values from -6 to 6
- step_raw: float32 [1536, 256], P('ctx', 'head'), may hold values from -13.5 to -1
- decay_log: float32 [256], P('head'), may hold values from -0.5 to 1
- b_proj: bfloat16 [1536, 1024], P('ctx', 'head'), may hold values from -6 to 6
- c_proj: bfloat16 [1536, 1024], P('ctx', 'head'), may hold values from -6 to 6
- mixer_grad: bfloat16 [1536, 16384], P('ctx', 'head'), may hold values from -6 to 6
- queries: bfloat16 [1536, 4096], P(('ctx', 'head')), may hold values from -200 to 200
- keys_in: bfloat16 [1536, 1024], P(('ctx', 'head')), may hold values from -6 to 6
- values: bfloat16 [1536, 1024], P(('ctx', 'head')), may hold values from -6 to 6
- out_grad: bfloat16 [1536, 4096], P(('ctx', 'head')), may hold values from -6 to 6
Outputs:
- grad_input: bfloat16 [1536, 16384], P('ctx', 'head')
- grad_step: float32 [1536, 256], P('ctx', 'head')
- grad_bproj: float32 [1536, 1024], P('ctx', 'head')
- grad_cproj: float32 [1536, 1024], P('ctx', 'head')
- grad_query: bfloat16 [1536, 4096], P(('ctx', 'head'))
- grad_key: bfloat16 [1536, 1024], P(('ctx', 'head'))
- grad_value: bfloat16 [1536, 1024], P(('ctx', 'head'))
The draws below stay inside these ranges and needn't reach their ends.
All inputs are finite; a program needn't handle non-finite values.
Results may differ from the reference program's by a relative error of at most 0.012.
Values may be sent and summed in bfloat16 or wider, within the bound.
A program may use at most 128 MiB of HBM per device.

```python
import math
import jax
import jax.numpy as jnp
from jax import lax

MAMBA_HEADS = 256
HEAD_P = 64
STATE = 128
GROUPS = 8
QHEADS = 32
KV_HEADS = 8
HEAD_DIM = 128
TOK_CTX = 192
SEQUENCE_TOKENS = 1536


def draw_step_raw(key, part):
    key_slow = jax.random.fold_in(key, 201)
    key_low = jax.random.fold_in(key, 202)
    key_high = jax.random.fold_in(key, 203)
    key_block = jax.random.fold_in(key, 204)
    key_rough = jax.random.fold_in(key, 205)
    key_span_group = jax.random.fold_in(key, 206)
    key_stride = jax.random.fold_in(key, 207)
    slow_share = 0.5
    slow_heads = jax.random.uniform(key_slow, (MAMBA_HEADS,), jnp.float32) < slow_share
    slow_rate = jnp.exp(jax.random.uniform(key_low, (MAMBA_HEADS,), jnp.float32, math.log(1e-05), math.log(6e-05)))
    fast_rate = jnp.exp(jax.random.uniform(key_high, (MAMBA_HEADS,), jnp.float32, math.log(0.003), math.log(0.025)))
    level = jnp.where(slow_heads, slow_rate, fast_rate)
    block_factor = jnp.exp(jax.random.uniform(key_block, (SEQUENCE_TOKENS // TOK_CTX, MAMBA_HEADS), jnp.float32, math.log(0.5), math.log(2.0)))
    roughness = jnp.exp(jax.random.uniform(key_rough, (SEQUENCE_TOKENS, MAMBA_HEADS), jnp.float32, math.log(0.6), math.log(1.6)))
    stride_length = level[None, :] * jnp.repeat(block_factor, TOK_CTX, axis=0) * roughness
    span_group_rows = jax.random.randint(key_span_group, (3,), 0, SEQUENCE_TOKENS)
    group_span_mask = jnp.any(jnp.arange(SEQUENCE_TOKENS)[:, None] == span_group_rows[None, :], axis=1)
    span_group_size = jax.random.uniform(key_stride, (MAMBA_HEADS,), jnp.float32, 0.15, 0.3)
    stride_length = jnp.where(group_span_mask[:, None], span_group_size[None, :], stride_length)
    return jnp.log(jnp.expm1(stride_length))


def paired_draw(key):
    key_keys = jax.random.fold_in(key, 301)
    key_query = jax.random.fold_in(key, 302)
    group_size = QHEADS // KV_HEADS
    base_keys = jnp.clip(jax.random.normal(key_keys, (SEQUENCE_TOKENS, KV_HEADS, HEAD_DIM), jnp.float32), -6.0, 6.0)
    base_query = jnp.clip(jax.random.normal(key_query, (SEQUENCE_TOKENS, KV_HEADS, group_size, HEAD_DIM), jnp.float32), -6.0, 6.0)
    return (base_query.reshape(SEQUENCE_TOKENS, QHEADS * HEAD_DIM), base_keys.reshape(SEQUENCE_TOKENS, KV_HEADS * HEAD_DIM))


def draw_queries(key, part):
    return paired_draw(jax.random.fold_in(key, 77))[0].astype(jnp.bfloat16)


def draw_keys_in(key, part):
    return paired_draw(jax.random.fold_in(key, 77))[1].astype(jnp.bfloat16)


def block_levels(stream_key, shape, cuts, low, top_value):
    level, own = 1.0, jax.random.fold_in(stream_key, 6)
    for dim, shards_of in cuts:
        draws = jnp.exp(jax.random.uniform(jax.random.fold_in(own, dim), (shards_of,), jnp.float32, low / len(cuts), top_value / len(cuts)))
        level = level * jnp.repeat(draws, shape[dim] // shards_of).reshape([-1 if axis == dim else 1 for axis in range(len(shape))])
    return level


def gaussian(key, extent, width, limit, split=(), dtype=jnp.bfloat16):
    result = jax.random.normal(key, extent, jnp.float32) * width
    if len(split) > 0:
        result = block_levels(key, extent, split, -0.22, 0.18) * result
    return jnp.clip(result, min=-limit, max=limit).astype(dtype)


def setup_inputs(seed: int = 0) -> dict:
    seeds = jax.random.split(jax.random.key(seed), 11)
    return {
        "mixer_in": gaussian(seeds[0], (SEQUENCE_TOKENS, MAMBA_HEADS * HEAD_P), 1.0, 6.0, ((0, 8), (1, 4))),
        "step_raw": draw_step_raw(jax.random.fold_in(seeds[10], 71), 0),
        "decay_log": jnp.clip(-0.5 + 1.5 * jax.random.uniform(seeds[2], (MAMBA_HEADS,), jnp.float32) ** block_levels(seeds[2], (MAMBA_HEADS,), ((0, 4),), -0.2, 0.2), -0.5, 1.0),
        "b_proj": gaussian(seeds[3], (SEQUENCE_TOKENS, GROUPS * STATE), 1.0, 6.0, ((0, 8), (1, 4))),
        "c_proj": gaussian(seeds[4], (SEQUENCE_TOKENS, GROUPS * STATE), 1.0, 6.0, ((0, 8), (1, 4))),
        "mixer_grad": gaussian(seeds[5], (SEQUENCE_TOKENS, MAMBA_HEADS * HEAD_P), 1.0, 6.0, ((0, 8), (1, 4))),
        "queries": draw_queries(jax.random.fold_in(seeds[10], 71), 0),
        "keys_in": draw_keys_in(jax.random.fold_in(seeds[10], 71), 0),
        "values": gaussian(seeds[8], (SEQUENCE_TOKENS, KV_HEADS * HEAD_DIM), 1.0, 6.0, ((0, 32),)),
        "out_grad": gaussian(seeds[9], (SEQUENCE_TOKENS, QHEADS * HEAD_DIM), 1.0, 6.0, ((0, 32),)),
    }


precise = lax.Precision.HIGHEST

def rounded(value):
    return lax.optimization_barrier(value.astype(jnp.bfloat16)).astype(jnp.float32)

def span_forward(inputs_f32, step_raw, decay_log, b_f32, c_f32, state_in):
    length, head_count, head_width = inputs_f32.shape
    groups = b_f32.shape[1]
    state_width = b_f32.shape[2]
    per_group = head_count // groups
    stride_length = jax.nn.softplus(step_raw)
    log_step = -jnp.exp(decay_log)[None, :] * stride_length
    cumulative = jnp.cumsum(log_step, axis=0)
    scaled = inputs_f32 * stride_length[:, :, None]
    gram_matrix = jnp.einsum('tgn,sgn->gts', c_f32, b_f32, precision=precise)
    causal = jnp.tril(jnp.ones((length, length), jnp.float32))
    cumul_rows = cumulative.T
    spread = cumul_rows[:, :, None] - cumul_rows[:, None, :]
    weights = jnp.exp(jnp.where(causal > 0.5, spread, 0.0)) * causal
    weights = weights.reshape(groups, per_group, length, length) * gram_matrix[:, None]
    scaled_grouped = scaled.reshape(length, groups, per_group, head_width)
    intra_term = jnp.einsum('gkts,sgkp->tgkp', weights, scaled_grouped, precision=precise)
    growth = jnp.exp(cumulative).reshape(length, groups, per_group)
    c_decay = c_f32[:, :, None, :] * growth[..., None]
    state_grouped = state_in.reshape(groups, per_group, head_width, state_width)
    inter_term = jnp.einsum('tgkn,gkpn->tgkp', c_decay, state_grouped, precision=precise)
    output = (intra_term + inter_term).reshape(length, head_count * head_width)
    tail_decay = jnp.exp(cumulative[-1][None, :] - cumulative).reshape(length, groups, per_group)
    carried = scaled_grouped * tail_decay[..., None]
    fresh_state = jnp.einsum('sgkp,sgn->gkpn', carried, b_f32, precision=precise)
    state_out = fresh_state.reshape(head_count, head_width, state_width) + jnp.exp(cumulative[-1])[:, None, None] * state_in
    return (output, state_out)

def mixer_forward(inputs_f32, step_raw, decay_log, bproj_f32, cproj_f32):
    block_count = SEQUENCE_TOKENS // TOK_CTX
    input_blocks = inputs_f32.reshape(block_count, TOK_CTX, MAMBA_HEADS, HEAD_P)
    step_blocks = step_raw.reshape(block_count, TOK_CTX, MAMBA_HEADS)
    b_blocks = bproj_f32.reshape(block_count, TOK_CTX, GROUPS, STATE)
    c_blocks = cproj_f32.reshape(block_count, TOK_CTX, GROUPS, STATE)

    def advance(state_now, pieces):
        output, state_next = span_forward(pieces[0], pieces[1], decay_log, pieces[2], pieces[3], state_now)
        return (state_next, output)
    initial = jnp.zeros((MAMBA_HEADS, HEAD_P, STATE), jnp.float32)
    unused, outputs = lax.scan(jax.checkpoint(advance), initial, (input_blocks, step_blocks, b_blocks, c_blocks))
    return outputs.reshape(SEQUENCE_TOKENS, MAMBA_HEADS * HEAD_P)

def attention_grads(queries, keys_in, values, out_grad):
    group_size = QHEADS // KV_HEADS
    factor = HEAD_DIM ** (-0.5)
    query_heads = queries.astype(jnp.float32).reshape(SEQUENCE_TOKENS, KV_HEADS, group_size, HEAD_DIM)
    grad_heads = out_grad.astype(jnp.float32).reshape(SEQUENCE_TOKENS, KV_HEADS, group_size, HEAD_DIM)
    key_heads = keys_in.astype(jnp.float32).reshape(SEQUENCE_TOKENS, KV_HEADS, HEAD_DIM)
    value_heads = values.astype(jnp.float32).reshape(SEQUENCE_TOKENS, KV_HEADS, HEAD_DIM)
    key_sum = jnp.zeros((SEQUENCE_TOKENS, KV_HEADS, HEAD_DIM), jnp.float32)
    value_sum = jnp.zeros((SEQUENCE_TOKENS, KV_HEADS, HEAD_DIM), jnp.float32)
    query_parts = []
    for block_start in range(0, SEQUENCE_TOKENS, TOK_CTX):
        block_end = block_start + TOK_CTX
        query_block = query_heads[block_start:block_end]
        grad_block = grad_heads[block_start:block_end]
        key_seen = key_heads[:block_end]
        value_seen = value_heads[:block_end]
        scores = jnp.einsum('tkgd,skd->kgts', query_block, key_seen) * factor
        query_pos = block_start + jnp.arange(TOK_CTX)
        visible = query_pos[:, None] >= jnp.arange(block_end)[None, :]
        scores = jnp.where(visible, scores, -jnp.inf)
        top_score = lax.optimization_barrier(jnp.max(scores, axis=-1, keepdims=True))
        log_norm = top_score + jnp.log(lax.optimization_barrier(jnp.sum(jnp.exp(scores - top_score), axis=-1, keepdims=True)))
        probs_f = jnp.exp(scores - log_norm)
        grad_prob = jnp.einsum('tkgd,skd->kgts', grad_block, value_seen)
        row_dot = lax.optimization_barrier(jnp.sum(probs_f * grad_prob, axis=-1, keepdims=True))
        grad_scores = probs_f * (grad_prob - row_dot)
        probs_b = rounded(probs_f)
        grad_b = rounded(grad_scores)
        query_parts.append(factor * jnp.einsum('kgts,skd->tkgd', grad_b, key_seen))
        key_sum = key_sum.at[:block_end].add(factor * jnp.einsum('kgts,tkgd->skd', grad_b, query_block))
        value_sum = value_sum.at[:block_end].add(jnp.einsum('kgts,tkgd->skd', probs_b, grad_block))
    grad_query = jnp.concatenate(query_parts, axis=0).reshape(SEQUENCE_TOKENS, QHEADS * HEAD_DIM).astype(jnp.bfloat16)
    grad_key = key_sum.reshape(SEQUENCE_TOKENS, KV_HEADS * HEAD_DIM).astype(jnp.bfloat16)
    grad_value = value_sum.reshape(SEQUENCE_TOKENS, KV_HEADS * HEAD_DIM).astype(jnp.bfloat16)
    return (grad_query, grad_key, grad_value)

def reference(mixer_in, step_raw, decay_log, b_proj, c_proj, mixer_grad, queries, keys_in, values, out_grad):

    def mixer_only(inputs_f32, step_part, bproj_f32, cproj_f32):
        return mixer_forward(inputs_f32, step_part, decay_log, bproj_f32, cproj_f32)
    primal, pullback = jax.vjp(mixer_only, mixer_in.astype(jnp.float32), step_raw, b_proj.astype(jnp.float32), c_proj.astype(jnp.float32))
    grads = pullback(mixer_grad.astype(jnp.float32))
    grad_query, grad_key, grad_value = attention_grads(queries, keys_in, values, out_grad)
    return (grads[0].astype(jnp.bfloat16), grads[1], grads[2], grads[3], grad_query, grad_key, grad_value)
```

```python
import functools

import jax
import jax.numpy as jnp
from jax import lax
from jax.experimental import pallas as pl
from jax.experimental.pallas import tpu as pltpu
from jax.sharding import PartitionSpec as P

STATE = 128
QHEADS = 32
KV_HEADS = 8
HEAD_DIM = 128
SUB = 64
GROUP = QHEADS // KV_HEADS
F32 = jnp.float32
BF = jnp.bfloat16


def mm(a, b, ca=1, cb=0, precision=None):
    return lax.dot_general(
        a, b, (((ca,), (cb,)), ((), ())), preferred_element_type=F32, precision=precision
    )


def split(v):
    hi = v.astype(BF)
    return hi, (v - hi.astype(F32)).astype(BF)


def body(
    nc, nh, tile,
    x_ref, step_ref, decay_ref, b_ref, c_ref, dy_ref, q_ref, k_ref, v_ref, o_ref,
    gx_ref, gs_ref, gb_ref, gc_ref, gq_ref, gk_ref, gv_ref,
    qbuf, obuf, kbuf, vbuf, kv, dkv, dkvin, kvb, q4, o4, dqb,
    s_scr, dp_scr,
    sloc, srecv, sin, decloc, decrecv,
    vec_hi, vec_lo, xt_scr, dyg_scr, gm, gmt, dg, acc, dbc,
    h_send, h_recv, kv_send, kv_recv, st_send, st_recv, dc_send, dc_recv,
    bk_send, bk_recv, dkv_send, dkv_recv, back_send, back_recv,
):
    L, CH = x_ref.shape
    H = step_ref.shape[1]
    width = CH // H
    groups = b_ref.shape[1] // STATE
    rows = q_ref.shape[0]
    qc = q_ref.shape[1] // nh
    kc = k_ref.shape[1] // nh
    nkv = kc // HEAD_DIM
    chunk = CH // nc
    per = tile // chunk
    tpg = CH // groups // tile
    nsub = L // SUB
    me = lax.axis_index("ctx")
    mh = lax.axis_index("head")
    factor = HEAD_DIM ** (-0.5)

    barrier = pltpu.get_barrier_semaphore()
    for d in range(1, nc):
        pl.semaphore_signal(barrier, inc=1, device_id={"ctx": lax.rem(me + d, nc)},
                            device_id_type=pl.DeviceIdType.MESH)
    for d in range(1, nh):
        pl.semaphore_signal(barrier, inc=1, device_id={"head": lax.rem(mh + d, nh)},
                            device_id_type=pl.DeviceIdType.MESH)
    pl.semaphore_wait(barrier, nc - 1 + nh - 1)

    def remote(src, dst, ss, rs, axis, peer):
        return pltpu.make_async_remote_copy(
            src_ref=src, dst_ref=dst, send_sem=ss, recv_sem=rs,
            device_id={axis: peer}, device_id_type=pl.DeviceIdType.MESH)

    def cols(ref, at, n):
        return ref.at[:, pl.ds(pl.multiple_of(at * n, 128), n)]

    head_copies = []
    for n, (ref, buf, w) in enumerate(
        ((k_ref, kbuf, kc), (v_ref, vbuf, kc), (q_ref, qbuf, qc), (o_ref, obuf, qc))):
        for d in range(1, nh):
            peer = lax.rem(mh + d, nh)
            cp = remote(cols(ref, peer, w), buf.at[mh], h_send.at[n, d], h_recv.at[n, d], "head", peer)
            cp.start()
            head_copies.append(cp)
    for ref, buf, w in ((k_ref, kbuf, kc), (v_ref, vbuf, kc), (q_ref, qbuf, qc), (o_ref, obuf, qc)):
        buf[mh] = ref[:, pl.ds(pl.multiple_of(mh * w, 128), w)]

    high = lax.Precision.HIGHEST
    raw = step_ref[...]
    e = jnp.exp(raw)
    dt = jnp.log1p(e)
    rate = jnp.exp(decay_ref[...])
    ri = lax.broadcasted_iota(jnp.int32, (L, L), 0)
    ci = lax.broadcasted_iota(jnp.int32, (L, L), 1)
    tril = (ri >= ci).astype(F32)
    cum = mm(tril, -rate * dt, precision=high)
    last = cum[L - 1:L]
    refs = [jnp.zeros((1, H), F32)] + [cum[SUB * i - 1:SUB * i] for i in range(1, nsub)]
    a = jnp.concatenate([jnp.exp(cum[SUB * i:SUB * (i + 1)] - refs[i]) for i in range(nsub)], 0)
    vecs = [dt, a, jnp.exp(cum), jnp.exp(last - cum)]
    for i in range(nsub):
        vecs.append(jnp.exp(refs[i] - cum[:SUB * (i + 1)]))
    vecs.append(jnp.broadcast_to(jnp.exp(last), (16, H)))
    offs = []
    at = 0
    for v in vecs:
        hi, lo = split(v)
        offs.append((at, v.shape[0]))
        vec_hi[at:at + v.shape[0]] = hi
        vec_lo[at:at + v.shape[0]] = lo
        at += v.shape[0]

    def spread_of(t):
        hr = lax.broadcasted_iota(jnp.int32, (H, tile), 0)
        hc = lax.broadcasted_iota(jnp.int32, (H, tile), 1)
        one = (hc // width + t * (tile // width) == hr).astype(F32).astype(BF)

        def get(n):
            o, r = offs[n]
            return mm(vec_hi[o:o + r], one) + mm(vec_lo[o:o + r], one)
        return get

    def gather_of(t):
        hr = lax.broadcasted_iota(jnp.int32, (tile, H), 0)
        hc = lax.broadcasted_iota(jnp.int32, (tile, H), 1)
        one = (hr // width + t * (tile // width) == hc).astype(F32).astype(BF)

        def put(v):
            hi, lo = split(v)
            return mm(hi, one) + mm(lo, one)
        return put

    DT, AA, GROW, TAIL, B0 = 0, 1, 2, 3, 4
    DEC = B0 + nsub

    for g in range(groups):
        bg = b_ref[:, g * STATE:(g + 1) * STATE]
        cg = c_ref[:, g * STATE:(g + 1) * STATE]

        def summary(k, carry):
            t = g * tpg + k
            here = pl.ds(pl.multiple_of(t * tile, 128), tile)
            get = spread_of(t)
            xt = (x_ref[:, here].astype(F32) * get(DT) * get(TAIL)).astype(BF)
            dyg = (dy_ref[:, here].astype(F32) * get(GROW)).astype(BF)
            xt_scr[:, here] = xt
            dyg_scr[:, here] = dyg
            st = mm(bg, xt, 0, 0).astype(BF)
            pu = mm(cg, dyg, 0, 0).astype(BF)
            de = get(DEC)[:8]
            for m in range(per):
                part = slice(m * chunk, (m + 1) * chunk)
                sloc[t * per + m, 0] = st[:, part]
                sloc[t * per + m, 1] = pu[:, part]
                decloc[t * per + m] = de[:, part]
            return carry

        lax.fori_loop(0, tpg, summary, 0)

    st_copies = []
    for d in range(1, nc):
        peer = lax.rem(me + d, nc)
        for cp in (
            remote(decloc.at[peer], decrecv.at[me], dc_send.at[d], dc_recv.at[d], "ctx", peer),
            remote(sloc.at[peer], srecv.at[me], st_send.at[d], st_recv.at[d], "ctx", peer)):
            cp.start()
            st_copies.append(cp)
    srecv[me] = sloc[me]
    decrecv[me] = decloc[me]

    for cp in head_copies[:2 * (nh - 1)]:
        cp.wait_recv()
    for h in range(nh):
        kv[me, h, :, :kc] = kbuf[h]
        kv[me, h, :, kc:] = vbuf[h]

    def kv_copy(d):
        return remote(kv.at[me], kv.at[me], kv_send.at[d], kv_recv.at[d], "ctx", lax.rem(me + d, nc))

    for d in range(1, nc):
        @pl.when(me + d < nc)
        def _():
            kv_copy(d).start()

    for cp in head_copies[2 * (nh - 1):]:
        cp.wait_recv()
    for src, dst in ((qbuf, q4), (obuf, o4)):
        for k in range(nkv):
            for i in range(GROUP):
                for h in range(nh):
                    c0 = (k * GROUP + i) * HEAD_DIM
                    dst[k, i * L + h * rows:i * L + (h + 1) * rows] = src[h, :, c0:c0 + HEAD_DIM]

    for cp in st_copies:
        cp.wait()

    def prefix(n, run):
        sloc[n, 0] = run.astype(BF)
        return decrecv[n][:1] * run + srecv[n, 0].astype(F32)

    def suffix(n, run):
        n = nc - 1 - n
        sloc[n, 1] = run.astype(BF)
        return decrecv[n][:1] * run + srecv[n, 1].astype(F32)

    lax.fori_loop(0, nc, prefix, jnp.zeros((STATE, chunk), F32))
    lax.fori_loop(0, nc, suffix, jnp.zeros((STATE, chunk), F32))
    bk_copies = []
    for d in range(1, nc):
        peer = lax.rem(me + d, nc)
        cp = remote(sloc.at[peer], sin.at[me], bk_send.at[d], bk_recv.at[d], "ctx", peer)
        cp.start()
        bk_copies.append(cp)
    sin[me] = sloc[me]

    for d in range(1, nc):
        @pl.when(me - d >= 0)
        def _():
            kv_copy(d).wait_recv()

    Q = GROUP * L
    key_row = lax.broadcasted_iota(jnp.int32, (L, L), 0)
    qry = lax.broadcasted_iota(jnp.int32, (L, L), 1)
    diag = jnp.where(qry >= key_row, 0.0, -jnp.inf).astype(F32)
    diag4 = jnp.concatenate([diag] * GROUP, 1)

    for k in range(nkv):
        kcol = slice(k * HEAD_DIM, (k + 1) * HEAD_DIM)
        vcol = slice(kc + k * HEAD_DIM, kc + (k + 1) * HEAD_DIM)

        def kblock(j):
            return kv[j, :, :, kcol].reshape(L, HEAD_DIM)

        def score(j, m):
            s = mm(kblock(j), q4[k], 1, 1) * factor
            s = s + jnp.where(j == me, diag4, 0.0)
            s_scr[j] = s
            dp_scr[j] = mm(kv[j, :, :, vcol].reshape(L, HEAD_DIM), o4[k], 1, 1)
            return jnp.maximum(m, jnp.max(s, 0, keepdims=True))

        top = lax.fori_loop(0, me + 1, score, jnp.full((1, Q), -jnp.inf, F32))

        def total(j, c):
            p = jnp.exp(s_scr[j] - top)
            s_scr[j] = p
            return (c[0] + jnp.sum(p, 0, keepdims=True),
                    c[1] + jnp.sum(p * dp_scr[j], 0, keepdims=True))

        z = jnp.zeros((1, Q), F32)
        norm, dot = lax.fori_loop(0, me + 1, total, (z, z))
        inv = 1.0 / norm
        dot = dot * inv

        def grads(j, dqt):
            p = s_scr[j] * inv
            ds = (p * (dp_scr[j] - dot)).astype(BF)
            dkv[j, :, kcol] = (factor * mm(ds, q4[k])).astype(BF)
            dkv[j, :, vcol] = mm(p.astype(BF), o4[k]).astype(BF)
            return dqt + mm(kblock(j), ds, 0, 0)

        dqt = lax.fori_loop(0, me + 1, grads, jnp.zeros((HEAD_DIM, Q), F32))
        dq = (factor * dqt).T.astype(BF)
        for i in range(GROUP):
            for h in range(nh):
                c0 = (k * GROUP + i) * HEAD_DIM
                dqb[h, :, c0:c0 + HEAD_DIM] = dq[i * L + h * rows:i * L + (h + 1) * rows]

    def dkv_copy(d):
        peer = lax.rem(me - d + nc, nc)
        return remote(dkv.at[peer], dkvin.at[d], dkv_send.at[d], dkv_recv.at[d], "ctx", peer)

    for d in range(1, nc):
        @pl.when(me - d >= 0)
        def _():
            dkv_copy(d).start()
    back = []
    for d in range(1, nh):
        peer = lax.rem(mh + d, nh)
        cp = remote(dqb.at[peer], cols(gq_ref, mh, qc), back_send.at[0, d], back_recv.at[0, d], "head", peer)
        cp.start()
        back.append(cp)
    gq_ref[:, pl.ds(pl.multiple_of(mh * qc, 128), qc)] = dqb[mh]

    causal = ri >= ci
    for g in range(groups):
        bg = b_ref[:, g * STATE:(g + 1) * STATE]
        cg = c_ref[:, g * STATE:(g + 1) * STATE]
        gm[g] = jnp.where(causal, mm(cg, bg, 1, 1), 0.0).astype(BF)
        full = jnp.where(ri <= ci, mm(bg, cg, 1, 1), 0.0).astype(BF)
        for i in range(nsub):
            gmt[g, i] = full[:, i * SUB:(i + 1) * SUB]
    dg[...] = jnp.zeros_like(dg)
    acc[...] = jnp.zeros_like(acc)
    dbc[...] = jnp.zeros_like(dbc)
    for cp in bk_copies:
        cp.wait_recv()

    is_last = lax.broadcasted_iota(jnp.int32, (L, tile), 0) == L - 1
    for g in range(groups):
        bg = b_ref[:, g * STATE:(g + 1) * STATE]
        cg = c_ref[:, g * STATE:(g + 1) * STATE]

        def main(k, carry):
            t = g * tpg + k
            here = pl.ds(pl.multiple_of(t * tile, 128), tile)
            get = spread_of(t)
            put = gather_of(t)
            s_in = jnp.concatenate([sin[t * per + m, 0] for m in range(per)], 1)
            ds_in = jnp.concatenate([sin[t * per + m, 1] for m in range(per)], 1)
            x = x_ref[:, here].astype(F32)
            dy = dy_ref[:, here].astype(F32)
            dte = get(DT)
            ae = get(AA)
            xs = x * dte
            ady = (ae * dy).astype(BF)
            xt = xt_scr[:, here]
            y_in = get(GROW) * mm(cg, s_in)
            bds = mm(bg, ds_in)
            ys = []
            dxs = get(TAIL) * bds
            for i in range(nsub):
                r = SUB * (i + 1)
                lo = SUB * i
                be = get(B0 + i)
                bx = (be * xs[:r]).astype(BF)
                ad = ady[lo:r]
                ys.append(ae[lo:r] * mm(gm[g, lo:r, :r], bx))
                add = be * mm(gmt[g, i, :r], ad)
                if r < L:
                    add = jnp.concatenate([add, jnp.zeros((L - r, tile), F32)], 0)
                dxs = dxs + add
                dg[g, lo:r, :r] += mm(ad, bx, 1, 1)
            y = y_in + jnp.concatenate(ys, 0)
            dbc[0, g] += mm(xt, ds_in, 1, 1)
            dbc[1, g] += mm(dyg_scr[:, here], s_in, 1, 1)
            gx_ref[:, here] = (dxs * dte).astype(BF)
            end = jnp.sum(xt.astype(F32) * bds, 0, keepdims=True) + get(DEC)[:1] * jnp.sum(
                s_in.astype(F32) * ds_in.astype(F32), 0, keepdims=True)
            acc[0] += put(dxs * x)
            acc[1] += put(dy * y + jnp.where(is_last, end, 0.0))
            return carry

        lax.fori_loop(0, tpg, main, 0)
        dgm = jnp.where(causal, dg[g], 0.0).astype(BF)
        gcols = slice(g * STATE, (g + 1) * STATE)
        gc_ref[:, gcols] = dbc[1, g] + mm(dgm, bg)
        gb_ref[:, gcols] = dbc[0, g] + mm(dgm, cg, 0, 0)

    direct = acc[0]
    dcum = acc[1] - dt * direct
    dell = mm((ri <= ci).astype(F32), dcum, precision=high)
    gs_ref[...] = (direct - rate * dell) * (e / (1.0 + e))

    for d in range(1, nc):
        @pl.when(me + d < nc)
        def _():
            dkv_copy(d).wait_recv()
    summed = lax.fori_loop(
        1, nc - me, lambda d, s: s + dkvin[d].astype(F32), dkv[me].astype(F32)).astype(BF)
    for h in range(nh):
        kvb[0, h] = summed[h * rows:(h + 1) * rows, :kc]
        kvb[1, h] = summed[h * rows:(h + 1) * rows, kc:]
    for n, ref in enumerate((gk_ref, gv_ref)):
        for d in range(1, nh):
            peer = lax.rem(mh + d, nh)
            cp = remote(kvb.at[n, peer], cols(ref, mh, kc), back_send.at[1 + n, d],
                        back_recv.at[1 + n, d], "head", peer)
            cp.start()
            back.append(cp)
        ref[:, pl.ds(pl.multiple_of(mh * kc, 128), kc)] = kvb[n, mh]
    for cp in back:
        cp.wait_recv()
    for cp in head_copies + bk_copies + back:
        cp.wait_send()
    for d in range(1, nc):
        @pl.when(me + d < nc)
        def _():
            kv_copy(d).wait_send()

        @pl.when(me - d >= 0)
        def _():
            dkv_copy(d).wait_send()


def per_device(nc, nh, *args):
    x, step, decay, b, c, dy, q, k, v, o = args
    L, CH = x.shape
    H = step.shape[1]
    groups = b.shape[1] // STATE
    rows = q.shape[0]
    qc = q.shape[1] // nh
    kc = k.shape[1] // nh
    nkv = kc // HEAD_DIM
    chunk = CH // nc
    tile = min(512, CH // groups)
    nsub = L // SUB
    vrows = 4 * L + sum(SUB * (i + 1) for i in range(nsub)) + 16
    vm = pl.BlockSpec(memory_space=pltpu.VMEM)
    sem = pltpu.SemaphoreType.DMA
    V = pltpu.VMEM
    scratch = [
        V((nh, rows, qc), BF), V((nh, rows, qc), BF), V((nh, rows, kc), BF), V((nh, rows, kc), BF),
        V((nc, nh, rows, 2 * kc), BF), V((nc, L, 2 * kc), BF), V((nc, L, 2 * kc), BF),
        V((2, nh, rows, kc), BF),
        V((nkv, GROUP * L, HEAD_DIM), BF), V((nkv, GROUP * L, HEAD_DIM), BF),
        V((nh, rows, qc), BF),
        V((nc, L, GROUP * L), F32), V((nc, L, GROUP * L), F32),
        V((nc, 2, STATE, chunk), BF), V((nc, 2, STATE, chunk), BF), V((nc, 2, STATE, chunk), BF),
        V((nc, 8, chunk), F32), V((nc, 8, chunk), F32),
        V((vrows, H), BF), V((vrows, H), BF),
        V((L, CH), BF), V((L, CH), BF),
        V((groups, L, L), BF), V((groups, nsub, L, SUB), BF), V((groups, L, L), F32),
        V((2, L, H), F32), V((2, groups, L, STATE), F32),
        sem((4, nh)), sem((4, nh)), sem((nc,)), sem((nc,)), sem((nc,)), sem((nc,)),
        sem((nc,)), sem((nc,)), sem((nc,)), sem((nc,)), sem((nc,)), sem((nc,)),
        sem((3, nh)), sem((3, nh)),
    ]
    outs = (
        jax.ShapeDtypeStruct(x.shape, BF), jax.ShapeDtypeStruct(step.shape, F32),
        jax.ShapeDtypeStruct(b.shape, F32), jax.ShapeDtypeStruct(c.shape, F32),
        jax.ShapeDtypeStruct(q.shape, BF), jax.ShapeDtypeStruct(k.shape, BF),
        jax.ShapeDtypeStruct(v.shape, BF),
    )
    return pl.pallas_call(
        functools.partial(body, nc, nh, tile),
        out_shape=outs,
        in_specs=[vm] * 10,
        out_specs=[vm] * 7,
        scratch_shapes=scratch,
        compiler_params=pltpu.CompilerParams(
            collective_id=0, has_side_effects=True, vmem_limit_bytes=63 * 1024 * 1024),
    )(x, step, decay.reshape(1, H), b, c, dy, q, k, v, o)


def solution(mesh):
    nc, nh = mesh.shape["ctx"], mesh.shape["head"]
    tok = P(("ctx", "head"), None)
    both = P("ctx", "head")
    return jax.shard_map(
        functools.partial(per_device, nc, nh),
        mesh=mesh,
        in_specs=(both, both, P("head"), both, both, both, tok, tok, tok, tok),
        out_specs=(both, both, both, both, tok, tok, tok),
        check_vma=False,
    )
```

```python
import functools

import jax
import jax.numpy as jnp
from jax import lax
from jax.experimental import pallas as pl
from jax.experimental.pallas import tpu as pltpu
from jax.sharding import PartitionSpec as P

STATE = 128
QHEADS = 32
KV_HEADS = 8
HEAD_DIM = 128
SUB = 64
GROUP = QHEADS // KV_HEADS
F32 = jnp.float32
BF = jnp.bfloat16


def mm(a, b, ca=1, cb=0, precision=None):
    return lax.dot_general(
        a, b, (((ca,), (cb,)), ((), ())), preferred_element_type=F32, precision=precision
    )


def split(v):
    hi = v.astype(BF)
    return hi, (v - hi.astype(F32)).astype(BF)


def body(
    nc, nh, tile,
    x_ref, step_ref, decay_ref, b_ref, c_ref, dy_ref, q_ref, k_ref, v_ref, o_ref,
    gx_ref, gs_ref, gb_ref, gc_ref, gq_ref, gk_ref, gv_ref,
    qbuf, obuf, kbuf, vbuf, kv, dkv, dkvin, kvb, q4, o4, dqb,
    s_scr, dp_scr,
    sloc, srecv, sin, decloc, decrecv,
    vec, xt_scr, dyg_scr, gm, gmt, dg, acc, dbc,
    h_send, h_recv, kv_send, kv_recv, st_send, st_recv, dc_send, dc_recv,
    bk_send, bk_recv, dkv_send, dkv_recv, back_send, back_recv,
):
    L, CH = x_ref.shape
    H = step_ref.shape[0]
    width = CH // H
    groups = b_ref.shape[1] // STATE
    rows = q_ref.shape[0]
    qc = q_ref.shape[1] // nh
    kc = k_ref.shape[1] // nh
    nkv = kc // HEAD_DIM
    chunk = CH // nc
    per = tile // chunk
    tpg = CH // groups // tile
    nsub = L // SUB
    me = lax.axis_index("ctx")
    mh = lax.axis_index("head")
    factor = HEAD_DIM ** (-0.5)

    barrier = pltpu.get_barrier_semaphore()
    for d in range(1, nc):
        pl.semaphore_signal(barrier, inc=1, device_id={"ctx": lax.rem(me + d, nc)},
                            device_id_type=pl.DeviceIdType.MESH)
    for d in range(1, nh):
        pl.semaphore_signal(barrier, inc=1, device_id={"head": lax.rem(mh + d, nh)},
                            device_id_type=pl.DeviceIdType.MESH)
    pl.semaphore_wait(barrier, nc - 1 + nh - 1)

    def remote(src, dst, ss, rs, axis, peer):
        return pltpu.make_async_remote_copy(
            src_ref=src, dst_ref=dst, send_sem=ss, recv_sem=rs,
            device_id={axis: peer}, device_id_type=pl.DeviceIdType.MESH)

    def cols(ref, at, n):
        return ref.at[:, pl.ds(pl.multiple_of(at * n, 128), n)]

    qk = qc // nkv
    moves = [(k_ref, kbuf, kc, 0, kc), (v_ref, vbuf, kc, 0, kc)]
    for k in range(nkv):
        moves += [(q_ref, qbuf.at[k], qc, k * qk, qk), (o_ref, obuf.at[k], qc, k * qk, qk)]

    def part_of(at, w, off, n):
        return pl.ds(pl.multiple_of(at * w + off, 128), n)

    head_copies = []
    for n, (ref, buf, w, off, size) in enumerate(moves):
        for d in range(1, nh):
            peer = lax.rem(mh + d, nh)
            cp = remote(ref.at[:, part_of(peer, w, off, size)], buf.at[mh],
                        h_send.at[n, d], h_recv.at[n, d], "head", peer)
            cp.start()
            head_copies.append(cp)
    for ref, buf, w, off, size in moves:
        buf[mh] = ref[:, part_of(mh, w, off, size)]

    high = lax.Precision.HIGHEST
    raw = step_ref[...].T
    e = jnp.exp(raw)
    dt = jnp.log1p(e)
    rate = jnp.exp(decay_ref[...])
    ri = lax.broadcasted_iota(jnp.int32, (L, L), 0)
    ci = lax.broadcasted_iota(jnp.int32, (L, L), 1)
    tril = (ri >= ci).astype(F32)
    cum = mm(tril, -rate * dt, precision=high)
    last = cum[L - 1:L]
    refs = [jnp.zeros((1, H), F32)] + [cum[SUB * i - 1:SUB * i] for i in range(1, nsub)]
    a = jnp.concatenate([jnp.exp(cum[SUB * i:SUB * (i + 1)] - refs[i]) for i in range(nsub)], 0)
    vecs = [dt, a, jnp.exp(cum), jnp.exp(last - cum)]
    for i in range(nsub):
        vecs.append(jnp.exp(refs[i] - cum[:SUB * (i + 1)]))
    vecs.append(jnp.broadcast_to(jnp.exp(last), (16, H)))
    offs = []
    at = 0
    for v in vecs:
        hi, lo = split(v)
        offs.append((at, v.shape[0]))
        vec[at:at + v.shape[0], :H] = hi
        vec[at:at + v.shape[0], H:] = lo
        at += v.shape[0]

    def spread_of(t):
        hr = lax.rem(lax.broadcasted_iota(jnp.int32, (2 * H, tile), 0), H)
        hc = lax.broadcasted_iota(jnp.int32, (2 * H, tile), 1)
        one = (hc // width + t * (tile // width) == hr).astype(F32).astype(BF)

        def get(n):
            o, r = offs[n]
            return mm(vec[o:o + r], one)
        return get

    def gather_of(t):
        hr = lax.broadcasted_iota(jnp.int32, (tile, H), 0)
        hc = lax.broadcasted_iota(jnp.int32, (tile, H), 1)
        one = (hr // width + t * (tile // width) == hc).astype(F32).astype(BF)

        def put(v):
            hi, lo = split(v)
            return mm(hi, one) + mm(lo, one)
        return put

    DT, AA, GROW, TAIL, B0 = 0, 1, 2, 3, 4
    DEC = B0 + nsub

    def kv_copy(d):
        return remote(kv.at[me], kv.at[me], kv_send.at[d], kv_recv.at[d], "ctx", lax.rem(me + d, nc))

    def send_kv():
        for cp in head_copies[:2 * (nh - 1)]:
            cp.wait_recv()
        for h in range(nh):
            kv[me, h, :, :kc] = kbuf[h]
            kv[me, h, :, kc:] = vbuf[h]
        for d in range(1, nc):
            @pl.when(me + d < nc)
            def _():
                kv_copy(d).start()

    for g in range(groups):
        bg = b_ref[:, g * STATE:(g + 1) * STATE]
        cg = c_ref[:, g * STATE:(g + 1) * STATE]

        def summary(k, carry):
            t = g * tpg + k
            here = pl.ds(pl.multiple_of(t * tile, 128), tile)
            get = spread_of(t)
            xt = (x_ref[:, here].astype(F32) * get(DT) * get(TAIL)).astype(BF)
            dyg = (dy_ref[:, here].astype(F32) * get(GROW)).astype(BF)
            xt_scr[:, here] = xt
            dyg_scr[:, here] = dyg
            st = mm(bg, xt, 0, 0).astype(BF)
            pu = mm(cg, dyg, 0, 0).astype(BF)
            de = get(DEC)[:8]
            for m in range(per):
                part = slice(m * chunk, (m + 1) * chunk)
                sloc[t * per + m, 0] = st[:, part]
                sloc[t * per + m, 1] = pu[:, part]
                decloc[t * per + m] = de[:, part]
            return carry

        lax.fori_loop(0, tpg, summary, 0)
        if g == 0:
            send_kv()

    st_copies = []
    for d in range(1, nc):
        peer = lax.rem(me + d, nc)
        for cp in (
            remote(decloc.at[peer], decrecv.at[me], dc_send.at[d], dc_recv.at[d], "ctx", peer),
            remote(sloc.at[peer], srecv.at[me], st_send.at[d], st_recv.at[d], "ctx", peer)):
            cp.start()
            st_copies.append(cp)
    srecv[me] = sloc[me]
    decrecv[me] = decloc[me]

    bk_copies = []

    def pass_states():
        for cp in st_copies:
            cp.wait()

        def prefix(n, run):
            sloc[n, 0] = run.astype(BF)
            return decrecv[n][:1] * run + srecv[n, 0].astype(F32)

        def suffix(n, run):
            n = nc - 1 - n
            sloc[n, 1] = run.astype(BF)
            return decrecv[n][:1] * run + srecv[n, 1].astype(F32)

        lax.fori_loop(0, nc, prefix, jnp.zeros((STATE, chunk), F32))
        lax.fori_loop(0, nc, suffix, jnp.zeros((STATE, chunk), F32))
        for d in range(1, nc):
            peer = lax.rem(me + d, nc)
            cp = remote(sloc.at[peer], sin.at[me], bk_send.at[d], bk_recv.at[d], "ctx", peer)
            cp.start()
            bk_copies.append(cp)
        sin[me] = sloc[me]

    for d in range(1, nc):
        @pl.when(me - d >= 0)
        def _():
            kv_copy(d).wait_recv()

    Q = GROUP * L
    key_row = lax.broadcasted_iota(jnp.int32, (L, L), 0)
    qry = lax.broadcasted_iota(jnp.int32, (L, L), 1)
    diag = jnp.where(qry >= key_row, 0.0, -jnp.inf).astype(F32)
    diag4 = jnp.concatenate([diag] * GROUP, 1)

    for k in range(nkv):
        for n in (2 + 2 * k, 3 + 2 * k):
            for cp in head_copies[n * (nh - 1):(n + 1) * (nh - 1)]:
                cp.wait_recv()
        for src, dst in ((qbuf, q4), (obuf, o4)):
            for i in range(GROUP):
                for h in range(nh):
                    dst[k, i * L + h * rows:i * L + (h + 1) * rows] = src[
                        k, h, :, i * HEAD_DIM:(i + 1) * HEAD_DIM]
        kcol = slice(k * HEAD_DIM, (k + 1) * HEAD_DIM)
        vcol = slice(kc + k * HEAD_DIM, kc + (k + 1) * HEAD_DIM)

        def kblock(j):
            return kv[j, :, :, kcol].reshape(L, HEAD_DIM)

        def score(j, m):
            s = mm(kblock(j), q4[k], 1, 1) * factor
            s = s + jnp.where(j == me, diag4, 0.0)
            s_scr[j] = s
            dp_scr[j] = mm(kv[j, :, :, vcol].reshape(L, HEAD_DIM), o4[k], 1, 1)
            return jnp.maximum(m, jnp.max(s, 0, keepdims=True))

        top = lax.fori_loop(0, me + 1, score, jnp.full((1, Q), -jnp.inf, F32))

        def total(j, c):
            p = jnp.exp(s_scr[j] - top)
            s_scr[j] = p
            return (c[0] + jnp.sum(p, 0, keepdims=True),
                    c[1] + jnp.sum(p * dp_scr[j], 0, keepdims=True))

        z = jnp.zeros((1, Q), F32)
        norm, dot = lax.fori_loop(0, me + 1, total, (z, z))
        inv = 1.0 / norm
        dot = dot * inv

        def grads(j, dqt):
            p = s_scr[j] * inv
            ds = (p * (dp_scr[j] - dot)).astype(BF)
            dkv[j, :, kcol] = (factor * mm(ds, q4[k])).astype(BF)
            dkv[j, :, vcol] = mm(p.astype(BF), o4[k]).astype(BF)
            return dqt + mm(kblock(j), ds, 0, 0)

        dqt = lax.fori_loop(0, me + 1, grads, jnp.zeros((HEAD_DIM, Q), F32))
        dq = (factor * dqt).T.astype(BF)
        for i in range(GROUP):
            for h in range(nh):
                c0 = (k * GROUP + i) * HEAD_DIM
                dqb[h, :, c0:c0 + HEAD_DIM] = dq[i * L + h * rows:i * L + (h + 1) * rows]
        if k == 0:
            pass_states()

    def dkv_copy(d):
        peer = lax.rem(me - d + nc, nc)
        return remote(dkv.at[peer], dkvin.at[d], dkv_send.at[d], dkv_recv.at[d], "ctx", peer)

    for d in range(1, nc):
        @pl.when(me - d >= 0)
        def _():
            dkv_copy(d).start()
    back = []
    for d in range(1, nh):
        peer = lax.rem(mh + d, nh)
        cp = remote(dqb.at[peer], cols(gq_ref, mh, qc), back_send.at[0, d], back_recv.at[0, d], "head", peer)
        cp.start()
        back.append(cp)
    gq_ref[:, pl.ds(pl.multiple_of(mh * qc, 128), qc)] = dqb[mh]

    causal = ri >= ci
    for g in range(groups):
        bg = b_ref[:, g * STATE:(g + 1) * STATE]
        cg = c_ref[:, g * STATE:(g + 1) * STATE]
        gm[g] = jnp.where(causal, mm(cg, bg, 1, 1), 0.0).astype(BF)
        full = jnp.where(ri <= ci, mm(bg, cg, 1, 1), 0.0).astype(BF)
        for i in range(nsub):
            gmt[g, i] = full[:, i * SUB:(i + 1) * SUB]
    dg[...] = jnp.zeros_like(dg)
    acc[...] = jnp.zeros_like(acc)
    dbc[...] = jnp.zeros_like(dbc)
    for cp in bk_copies:
        cp.wait_recv()

    def home():
        for d in range(1, nc):
            @pl.when(me + d < nc)
            def _():
                dkv_copy(d).wait_recv()
        summed = lax.fori_loop(
            1, nc - me, lambda d, s: s + dkvin[d].astype(F32), dkv[me].astype(F32)).astype(BF)
        for h in range(nh):
            kvb[0, h] = summed[h * rows:(h + 1) * rows, :kc]
            kvb[1, h] = summed[h * rows:(h + 1) * rows, kc:]
        for n, ref in enumerate((gk_ref, gv_ref)):
            for d in range(1, nh):
                peer = lax.rem(mh + d, nh)
                cp = remote(kvb.at[n, peer], cols(ref, mh, kc), back_send.at[1 + n, d],
                            back_recv.at[1 + n, d], "head", peer)
                cp.start()
                back.append(cp)
            ref[:, pl.ds(pl.multiple_of(mh * kc, 128), kc)] = kvb[n, mh]

    is_last = lax.broadcasted_iota(jnp.int32, (L, tile), 0) == L - 1
    for g in range(groups):
        bg = b_ref[:, g * STATE:(g + 1) * STATE]
        cg = c_ref[:, g * STATE:(g + 1) * STATE]

        def main(k, carry):
            t = g * tpg + k
            here = pl.ds(pl.multiple_of(t * tile, 128), tile)
            get = spread_of(t)
            put = gather_of(t)
            s_in = jnp.concatenate([sin[t * per + m, 0] for m in range(per)], 1)
            ds_in = jnp.concatenate([sin[t * per + m, 1] for m in range(per)], 1)
            x = x_ref[:, here].astype(F32)
            dy = dy_ref[:, here].astype(F32)
            dte = get(DT)
            ae = get(AA)
            xs = x * dte
            ady = (ae * dy).astype(BF)
            xt = xt_scr[:, here]
            y_in = get(GROW) * mm(cg, s_in)
            bds = mm(bg, ds_in)
            ys = []
            dxs = get(TAIL) * bds
            for i in range(nsub):
                r = SUB * (i + 1)
                lo = SUB * i
                be = get(B0 + i)
                bx = (be * xs[:r]).astype(BF)
                ad = ady[lo:r]
                ys.append(ae[lo:r] * mm(gm[g, lo:r, :r], bx))
                add = be * mm(gmt[g, i, :r], ad)
                if r < L:
                    add = jnp.concatenate([add, jnp.zeros((L - r, tile), F32)], 0)
                dxs = dxs + add
                dg[g, lo:r, :r] += mm(ad, bx, 1, 1)
            y = y_in + jnp.concatenate(ys, 0)
            dbc[0, g] += mm(xt, ds_in, 1, 1)
            dbc[1, g] += mm(dyg_scr[:, here], s_in, 1, 1)
            gx_ref[:, here] = (dxs * dte).astype(BF)
            end = jnp.sum(xt.astype(F32) * bds, 0, keepdims=True) + get(DEC)[:1] * jnp.sum(
                s_in.astype(F32) * ds_in.astype(F32), 0, keepdims=True)
            acc[0] += put(dxs * x)
            acc[1] += put(dy * y + jnp.where(is_last, end, 0.0))
            return carry

        lax.fori_loop(0, tpg, main, 0)
        if g == 0:
            home()
        dgm = jnp.where(causal, dg[g], 0.0).astype(BF)
        gcols = slice(g * STATE, (g + 1) * STATE)
        gc_ref[:, gcols] = dbc[1, g] + mm(dgm, bg)
        gb_ref[:, gcols] = dbc[0, g] + mm(dgm, cg, 0, 0)

    direct = acc[0]
    dcum = acc[1] - dt * direct
    dell = mm((ri <= ci).astype(F32), dcum, precision=high)
    gs_ref[...] = ((direct - rate * dell) * (e / (1.0 + e))).T

    for cp in back:
        cp.wait_recv()
    for cp in head_copies + bk_copies + back:
        cp.wait_send()
    for d in range(1, nc):
        @pl.when(me + d < nc)
        def _():
            kv_copy(d).wait_send()

        @pl.when(me - d >= 0)
        def _():
            dkv_copy(d).wait_send()


def per_device(nc, nh, *args):
    x, step, decay, b, c, dy, q, k, v, o = args
    L, CH = x.shape
    H = step.shape[1]
    groups = b.shape[1] // STATE
    rows = q.shape[0]
    qc = q.shape[1] // nh
    kc = k.shape[1] // nh
    nkv = kc // HEAD_DIM
    chunk = CH // nc
    tile = min(512, CH // groups)
    nsub = L // SUB
    vrows = 4 * L + sum(SUB * (i + 1) for i in range(nsub)) + 16
    vm = pl.BlockSpec(memory_space=pltpu.VMEM)
    sem = pltpu.SemaphoreType.DMA
    V = pltpu.VMEM
    scratch = [
        V((nkv, nh, rows, qc // nkv), BF), V((nkv, nh, rows, qc // nkv), BF), V((nh, rows, kc), BF), V((nh, rows, kc), BF),
        V((nc, nh, rows, 2 * kc), BF), V((nc, L, 2 * kc), BF), V((nc, L, 2 * kc), BF),
        V((2, nh, rows, kc), BF),
        V((nkv, GROUP * L, HEAD_DIM), BF), V((nkv, GROUP * L, HEAD_DIM), BF),
        V((nh, rows, qc), BF),
        V((nc, L, GROUP * L), F32), V((nc, L, GROUP * L), F32),
        V((nc, 2, STATE, chunk), BF), V((nc, 2, STATE, chunk), BF), V((nc, 2, STATE, chunk), BF),
        V((nc, 8, chunk), F32), V((nc, 8, chunk), F32),
        V((vrows, 2 * H), BF),
        V((L, CH), BF), V((L, CH), BF),
        V((groups, L, L), BF), V((groups, nsub, L, SUB), BF), V((groups, L, L), F32),
        V((2, L, H), F32), V((2, groups, L, STATE), F32),
        sem((2 + 2 * nkv, nh)), sem((2 + 2 * nkv, nh)), sem((nc,)), sem((nc,)), sem((nc,)), sem((nc,)),
        sem((nc,)), sem((nc,)), sem((nc,)), sem((nc,)), sem((nc,)), sem((nc,)),
        sem((3, nh)), sem((3, nh)),
    ]
    outs = (
        jax.ShapeDtypeStruct(x.shape, BF), jax.ShapeDtypeStruct((H, L), F32),
        jax.ShapeDtypeStruct(b.shape, F32), jax.ShapeDtypeStruct(c.shape, F32),
        jax.ShapeDtypeStruct(q.shape, BF), jax.ShapeDtypeStruct(k.shape, BF),
        jax.ShapeDtypeStruct(v.shape, BF),
    )
    res = pl.pallas_call(
        functools.partial(body, nc, nh, tile),
        out_shape=outs,
        in_specs=[vm] * 10,
        out_specs=[vm] * 7,
        scratch_shapes=scratch,
        compiler_params=pltpu.CompilerParams(
            collective_id=0, has_side_effects=True, vmem_limit_bytes=63 * 1024 * 1024),
    )(x, step.T, decay.reshape(1, H), b, c, dy, q, k, v, o)
    return (res[0], res[1].T) + tuple(res[2:])


def solution(mesh):
    nc, nh = mesh.shape["ctx"], mesh.shape["head"]
    tok = P(("ctx", "head"), None)
    both = P("ctx", "head")
    return jax.shard_map(
        functools.partial(per_device, nc, nh),
        mesh=mesh,
        in_specs=(both, both, P("head"), both, both, both, tok, tok, tok, tok),
        out_specs=(both, both, both, both, tok, tok, tok),
        check_vma=False,
    )
```

```python
import functools

import jax
import jax.numpy as jnp
from jax import lax
from jax.experimental import pallas as pl
from jax.experimental.pallas import tpu as pltpu
from jax.sharding import PartitionSpec as P

STATE = 128
QHEADS = 32
KV_HEADS = 8
HEAD_DIM = 128
SUB = 64
GROUP = QHEADS // KV_HEADS
F32 = jnp.float32
BF = jnp.bfloat16


def mm(a, b, ca=1, cb=0, precision=None):
    return lax.dot_general(
        a, b, (((ca,), (cb,)), ((), ())), preferred_element_type=F32, precision=precision
    )


def split(v):
    hi = v.astype(BF)
    return hi, (v - hi.astype(F32)).astype(BF)


def body(
    nc, nh, tile,
    x_ref, step_ref, decay_ref, b_ref, c_ref, dy_ref, q_ref, k_ref, v_ref, o_ref,
    gx_ref, gs_ref, gb_ref, gc_ref, gq_ref, gk_ref, gv_ref,
    qbuf, obuf, kbuf, vbuf, kv, dkv, dkvin, kvb, q4, o4, dqb,
    s_scr, dp_scr,
    sloc, srecv, sin, decloc, decrecv,
    vec, xt_scr, dyg_scr, gm, gmt, dg, acc, dbc,
    h_send, h_recv, kv_send, kv_recv, st_send, st_recv, dc_send, dc_recv,
    bk_send, bk_recv, dkv_send, dkv_recv, back_send, back_recv,
):
    L, CH = x_ref.shape
    H = step_ref.shape[0]
    width = CH // H
    groups = b_ref.shape[1] // STATE
    rows = q_ref.shape[0]
    qc = q_ref.shape[1] // nh
    kc = k_ref.shape[1] // nh
    nkv = kc // HEAD_DIM
    chunk = CH // nc
    per = tile // chunk
    tpg = CH // groups // tile
    nsub = L // SUB
    me = lax.axis_index("ctx")
    mh = lax.axis_index("head")
    factor = HEAD_DIM ** (-0.5)

    barrier = pltpu.get_barrier_semaphore()
    for d in range(1, nc):
        pl.semaphore_signal(barrier, inc=1, device_id={"ctx": lax.rem(me + d, nc)},
                            device_id_type=pl.DeviceIdType.MESH)
    for d in range(1, nh):
        pl.semaphore_signal(barrier, inc=1, device_id={"head": lax.rem(mh + d, nh)},
                            device_id_type=pl.DeviceIdType.MESH)
    pl.semaphore_wait(barrier, nc - 1 + nh - 1)

    def remote(src, dst, ss, rs, axis, peer):
        return pltpu.make_async_remote_copy(
            src_ref=src, dst_ref=dst, send_sem=ss, recv_sem=rs,
            device_id={axis: peer}, device_id_type=pl.DeviceIdType.MESH)

    def cols(ref, at, n):
        return ref.at[:, pl.ds(pl.multiple_of(at * n, 128), n)]

    qk = qc // nkv
    moves = [(k_ref, kbuf, kc, 0, kc), (v_ref, vbuf, kc, 0, kc)]
    for k in range(nkv):
        moves += [(q_ref, qbuf.at[k], qc, k * qk, qk), (o_ref, obuf.at[k], qc, k * qk, qk)]

    def part_of(at, w, off, n):
        return pl.ds(pl.multiple_of(at * w + off, 128), n)

    head_copies = []
    for n, (ref, buf, w, off, size) in enumerate(moves):
        for d in range(1, nh):
            peer = lax.rem(mh + d, nh)
            cp = remote(ref.at[:, part_of(peer, w, off, size)], buf.at[mh],
                        h_send.at[n, d], h_recv.at[n, d], "head", peer)
            cp.start()
            head_copies.append(cp)
    for ref, buf, w, off, size in moves:
        buf[mh] = ref[:, part_of(mh, w, off, size)]

    high = lax.Precision.HIGHEST
    raw = step_ref[...].T
    e = jnp.exp(raw)
    dt = jnp.log1p(e)
    rate = jnp.exp(decay_ref[...])
    ri = lax.broadcasted_iota(jnp.int32, (L, L), 0)
    ci = lax.broadcasted_iota(jnp.int32, (L, L), 1)
    tril = (ri >= ci).astype(F32)
    cum = mm(tril, -rate * dt, precision=high)
    last = cum[L - 1:L]
    refs = [jnp.zeros((1, H), F32)] + [cum[SUB * i - 1:SUB * i] for i in range(1, nsub)]
    a = jnp.concatenate([jnp.exp(cum[SUB * i:SUB * (i + 1)] - refs[i]) for i in range(nsub)], 0)
    vecs = [dt, a, jnp.exp(cum), jnp.exp(last - cum)]
    for i in range(nsub):
        vecs.append(jnp.exp(refs[i] - cum[:SUB * (i + 1)]))
    vecs.append(jnp.broadcast_to(jnp.exp(last), (16, H)))
    offs = []
    at = 0
    for v in vecs:
        hi, lo = split(v)
        offs.append((at, v.shape[0]))
        vec[at:at + v.shape[0], :H] = hi
        vec[at:at + v.shape[0], H:] = lo
        at += v.shape[0]

    def spread_of(t):
        hr = lax.rem(lax.broadcasted_iota(jnp.int32, (2 * H, tile), 0), H)
        hc = lax.broadcasted_iota(jnp.int32, (2 * H, tile), 1)
        one = (hc // width + t * (tile // width) == hr).astype(F32).astype(BF)

        def get(n):
            o, r = offs[n]
            return mm(vec[o:o + r], one)
        return get

    def gather_of(t):
        hr = lax.broadcasted_iota(jnp.int32, (tile, H), 0)
        hc = lax.broadcasted_iota(jnp.int32, (tile, H), 1)
        one = (hr // width + t * (tile // width) == hc).astype(F32).astype(BF)

        def put(v):
            hi, lo = split(v)
            return mm(hi, one) + mm(lo, one)
        return put

    DT, AA, GROW, TAIL, B0 = 0, 1, 2, 3, 4
    DEC = B0 + nsub

    def kv_copy(d):
        return remote(kv.at[me], kv.at[me], kv_send.at[d], kv_recv.at[d], "ctx", lax.rem(me + d, nc))

    def send_kv():
        for cp in head_copies[:2 * (nh - 1)]:
            cp.wait_recv()
        for h in range(nh):
            kv[me, h, :, :kc] = kbuf[h]
            kv[me, h, :, kc:] = vbuf[h]
        for d in range(1, nc):
            @pl.when(me + d < nc)
            def _():
                kv_copy(d).start()

    for g in range(groups):
        bg = b_ref[:, g * STATE:(g + 1) * STATE]
        cg = c_ref[:, g * STATE:(g + 1) * STATE]

        def summary(k, carry):
            t = g * tpg + k
            here = pl.ds(pl.multiple_of(t * tile, 128), tile)
            get = spread_of(t)
            xt = (x_ref[:, here].astype(F32) * get(DT) * get(TAIL)).astype(BF)
            dyg = (dy_ref[:, here].astype(F32) * get(GROW)).astype(BF)
            xt_scr[:, here] = xt
            dyg_scr[:, here] = dyg
            st = mm(bg, xt, 0, 0).astype(BF)
            pu = mm(cg, dyg, 0, 0).astype(BF)
            de = get(DEC)[:8]
            for m in range(per):
                part = slice(m * chunk, (m + 1) * chunk)
                sloc[t * per + m, 0] = st[:, part]
                sloc[t * per + m, 1] = pu[:, part]
                decloc[t * per + m] = de[:, part]
            return carry

        lax.fori_loop(0, tpg, summary, 0)

    st_copies = []
    for d in range(1, nc):
        peer = lax.rem(me + d, nc)
        for cp in (
            remote(decloc.at[peer], decrecv.at[me], dc_send.at[d], dc_recv.at[d], "ctx", peer),
            remote(sloc.at[peer], srecv.at[me], st_send.at[d], st_recv.at[d], "ctx", peer)):
            cp.start()
            st_copies.append(cp)
    srecv[me] = sloc[me]
    decrecv[me] = decloc[me]
    send_kv()

    bk_copies = []

    def pass_states():
        for cp in st_copies:
            cp.wait()

        def prefix(n, run):
            sloc[n, 0] = run.astype(BF)
            return decrecv[n][:1] * run + srecv[n, 0].astype(F32)

        def suffix(n, run):
            n = nc - 1 - n
            sloc[n, 1] = run.astype(BF)
            return decrecv[n][:1] * run + srecv[n, 1].astype(F32)

        lax.fori_loop(0, nc, prefix, jnp.zeros((STATE, chunk), F32))
        lax.fori_loop(0, nc, suffix, jnp.zeros((STATE, chunk), F32))
        for d in range(1, nc):
            peer = lax.rem(me + d, nc)
            cp = remote(sloc.at[peer], sin.at[me], bk_send.at[d], bk_recv.at[d], "ctx", peer)
            cp.start()
            bk_copies.append(cp)
        sin[me] = sloc[me]

    pass_states()

    for d in range(1, nc):
        @pl.when(me - d >= 0)
        def _():
            kv_copy(d).wait_recv()

    Q = GROUP * L
    key_row = lax.broadcasted_iota(jnp.int32, (L, L), 0)
    qry = lax.broadcasted_iota(jnp.int32, (L, L), 1)
    diag = jnp.where(qry >= key_row, 0.0, -jnp.inf).astype(F32)
    diag4 = jnp.concatenate([diag] * GROUP, 1)

    for k in range(nkv):
        for n in (2 + 2 * k, 3 + 2 * k):
            for cp in head_copies[n * (nh - 1):(n + 1) * (nh - 1)]:
                cp.wait_recv()
        for src, dst in ((qbuf, q4), (obuf, o4)):
            for i in range(GROUP):
                for h in range(nh):
                    dst[k, i * L + h * rows:i * L + (h + 1) * rows] = src[
                        k, h, :, i * HEAD_DIM:(i + 1) * HEAD_DIM]
        kcol = slice(k * HEAD_DIM, (k + 1) * HEAD_DIM)
        vcol = slice(kc + k * HEAD_DIM, kc + (k + 1) * HEAD_DIM)

        def kblock(j):
            return kv[j, :, :, kcol].reshape(L, HEAD_DIM)

        def score(j, m):
            s = mm(kblock(j), q4[k], 1, 1) * factor
            s = s + jnp.where(j == me, diag4, 0.0)
            s_scr[j] = s
            dp_scr[j] = mm(kv[j, :, :, vcol].reshape(L, HEAD_DIM), o4[k], 1, 1)
            return jnp.maximum(m, jnp.max(s, 0, keepdims=True))

        top = lax.fori_loop(0, me + 1, score, jnp.full((1, Q), -jnp.inf, F32))

        def total(j, c):
            p = jnp.exp(s_scr[j] - top)
            s_scr[j] = p
            return (c[0] + jnp.sum(p, 0, keepdims=True),
                    c[1] + jnp.sum(p * dp_scr[j], 0, keepdims=True))

        z = jnp.zeros((1, Q), F32)
        norm, dot = lax.fori_loop(0, me + 1, total, (z, z))
        inv = 1.0 / norm
        dot = dot * inv

        def grads(j, dqt):
            p = s_scr[j] * inv
            ds = (p * (dp_scr[j] - dot)).astype(BF)
            dkv[j, :, kcol] = (factor * mm(ds, q4[k])).astype(BF)
            dkv[j, :, vcol] = mm(p.astype(BF), o4[k]).astype(BF)
            return dqt + mm(kblock(j), ds, 0, 0)

        dqt = lax.fori_loop(0, me + 1, grads, jnp.zeros((HEAD_DIM, Q), F32))
        dq = (factor * dqt).T.astype(BF)
        for i in range(GROUP):
            for h in range(nh):
                c0 = (k * GROUP + i) * HEAD_DIM
                dqb[h, :, c0:c0 + HEAD_DIM] = dq[i * L + h * rows:i * L + (h + 1) * rows]

    def dkv_copy(d):
        peer = lax.rem(me - d + nc, nc)
        return remote(dkv.at[peer], dkvin.at[d], dkv_send.at[d], dkv_recv.at[d], "ctx", peer)

    for d in range(1, nc):
        @pl.when(me - d >= 0)
        def _():
            dkv_copy(d).start()
    back = []
    for d in range(1, nh):
        peer = lax.rem(mh + d, nh)
        cp = remote(dqb.at[peer], cols(gq_ref, mh, qc), back_send.at[0, d], back_recv.at[0, d], "head", peer)
        cp.start()
        back.append(cp)
    gq_ref[:, pl.ds(pl.multiple_of(mh * qc, 128), qc)] = dqb[mh]

    causal = ri >= ci
    for g in range(groups):
        bg = b_ref[:, g * STATE:(g + 1) * STATE]
        cg = c_ref[:, g * STATE:(g + 1) * STATE]
        gm[g] = jnp.where(causal, mm(cg, bg, 1, 1), 0.0).astype(BF)
        full = jnp.where(ri <= ci, mm(bg, cg, 1, 1), 0.0).astype(BF)
        for i in range(nsub):
            gmt[g, i] = full[:, i * SUB:(i + 1) * SUB]
    dg[...] = jnp.zeros_like(dg)
    acc[...] = jnp.zeros_like(acc)
    dbc[...] = jnp.zeros_like(dbc)
    for cp in bk_copies:
        cp.wait_recv()

    def home():
        for d in range(1, nc):
            @pl.when(me + d < nc)
            def _():
                dkv_copy(d).wait_recv()
        summed = lax.fori_loop(
            1, nc - me, lambda d, s: s + dkvin[d].astype(F32), dkv[me].astype(F32)).astype(BF)
        for h in range(nh):
            kvb[0, h] = summed[h * rows:(h + 1) * rows, :kc]
            kvb[1, h] = summed[h * rows:(h + 1) * rows, kc:]
        for n, ref in enumerate((gk_ref, gv_ref)):
            for d in range(1, nh):
                peer = lax.rem(mh + d, nh)
                cp = remote(kvb.at[n, peer], cols(ref, mh, kc), back_send.at[1 + n, d],
                            back_recv.at[1 + n, d], "head", peer)
                cp.start()
                back.append(cp)
            ref[:, pl.ds(pl.multiple_of(mh * kc, 128), kc)] = kvb[n, mh]

    is_last = lax.broadcasted_iota(jnp.int32, (L, tile), 0) == L - 1
    for g in range(groups):
        bg = b_ref[:, g * STATE:(g + 1) * STATE]
        cg = c_ref[:, g * STATE:(g + 1) * STATE]

        def main(k, carry):
            t = g * tpg + k
            here = pl.ds(pl.multiple_of(t * tile, 128), tile)
            get = spread_of(t)
            put = gather_of(t)
            s_in = jnp.concatenate([sin[t * per + m, 0] for m in range(per)], 1)
            ds_in = jnp.concatenate([sin[t * per + m, 1] for m in range(per)], 1)
            x = x_ref[:, here].astype(F32)
            dy = dy_ref[:, here].astype(F32)
            dte = get(DT)
            ae = get(AA)
            xs = x * dte
            ady = (ae * dy).astype(BF)
            xt = xt_scr[:, here]
            y_in = get(GROW) * mm(cg, s_in)
            bds = mm(bg, ds_in)
            ys = []
            dxs = get(TAIL) * bds
            for i in range(nsub):
                r = SUB * (i + 1)
                lo = SUB * i
                be = get(B0 + i)
                bx = (be * xs[:r]).astype(BF)
                ad = ady[lo:r]
                ys.append(ae[lo:r] * mm(gm[g, lo:r, :r], bx))
                add = be * mm(gmt[g, i, :r], ad)
                if r < L:
                    add = jnp.concatenate([add, jnp.zeros((L - r, tile), F32)], 0)
                dxs = dxs + add
                dg[g, lo:r, :r] += mm(ad, bx, 1, 1)
            y = y_in + jnp.concatenate(ys, 0)
            dbc[0, g] += mm(xt, ds_in, 1, 1)
            dbc[1, g] += mm(dyg_scr[:, here], s_in, 1, 1)
            gx_ref[:, here] = (dxs * dte).astype(BF)
            end = jnp.sum(xt.astype(F32) * bds, 0, keepdims=True) + get(DEC)[:1] * jnp.sum(
                s_in.astype(F32) * ds_in.astype(F32), 0, keepdims=True)
            acc[0] += put(dxs * x)
            acc[1] += put(dy * y + jnp.where(is_last, end, 0.0))
            return carry

        lax.fori_loop(0, tpg, main, 0)
        dgm = jnp.where(causal, dg[g], 0.0).astype(BF)
        gcols = slice(g * STATE, (g + 1) * STATE)
        gc_ref[:, gcols] = dbc[1, g] + mm(dgm, bg)
        gb_ref[:, gcols] = dbc[0, g] + mm(dgm, cg, 0, 0)

    direct = acc[0]
    dcum = acc[1] - dt * direct
    dell = mm((ri <= ci).astype(F32), dcum, precision=high)
    gs_ref[...] = ((direct - rate * dell) * (e / (1.0 + e))).T

    home()
    for cp in back:
        cp.wait_recv()
    for cp in head_copies + bk_copies + back:
        cp.wait_send()
    for d in range(1, nc):
        @pl.when(me + d < nc)
        def _():
            kv_copy(d).wait_send()

        @pl.when(me - d >= 0)
        def _():
            dkv_copy(d).wait_send()


def per_device(nc, nh, *args):
    x, step, decay, b, c, dy, q, k, v, o = args
    L, CH = x.shape
    H = step.shape[1]
    groups = b.shape[1] // STATE
    rows = q.shape[0]
    qc = q.shape[1] // nh
    kc = k.shape[1] // nh
    nkv = kc // HEAD_DIM
    chunk = CH // nc
    tile = min(512, CH // groups)
    nsub = L // SUB
    vrows = 4 * L + sum(SUB * (i + 1) for i in range(nsub)) + 16
    vm = pl.BlockSpec(memory_space=pltpu.VMEM)
    sem = pltpu.SemaphoreType.DMA
    V = pltpu.VMEM
    scratch = [
        V((nkv, nh, rows, qc // nkv), BF), V((nkv, nh, rows, qc // nkv), BF), V((nh, rows, kc), BF), V((nh, rows, kc), BF),
        V((nc, nh, rows, 2 * kc), BF), V((nc, L, 2 * kc), BF), V((nc, L, 2 * kc), BF),
        V((2, nh, rows, kc), BF),
        V((nkv, GROUP * L, HEAD_DIM), BF), V((nkv, GROUP * L, HEAD_DIM), BF),
        V((nh, rows, qc), BF),
        V((nc, L, GROUP * L), F32), V((nc, L, GROUP * L), F32),
        V((nc, 2, STATE, chunk), BF), V((nc, 2, STATE, chunk), BF), V((nc, 2, STATE, chunk), BF),
        V((nc, 8, chunk), F32), V((nc, 8, chunk), F32),
        V((vrows, 2 * H), BF),
        V((L, CH), BF), V((L, CH), BF),
        V((groups, L, L), BF), V((groups, nsub, L, SUB), BF), V((groups, L, L), F32),
        V((2, L, H), F32), V((2, groups, L, STATE), F32),
        sem((2 + 2 * nkv, nh)), sem((2 + 2 * nkv, nh)), sem((nc,)), sem((nc,)), sem((nc,)), sem((nc,)),
        sem((nc,)), sem((nc,)), sem((nc,)), sem((nc,)), sem((nc,)), sem((nc,)),
        sem((3, nh)), sem((3, nh)),
    ]
    outs = (
        jax.ShapeDtypeStruct(x.shape, BF), jax.ShapeDtypeStruct((H, L), F32),
        jax.ShapeDtypeStruct(b.shape, F32), jax.ShapeDtypeStruct(c.shape, F32),
        jax.ShapeDtypeStruct(q.shape, BF), jax.ShapeDtypeStruct(k.shape, BF),
        jax.ShapeDtypeStruct(v.shape, BF),
    )
    res = pl.pallas_call(
        functools.partial(body, nc, nh, tile),
        out_shape=outs,
        in_specs=[vm] * 10,
        out_specs=[vm] * 7,
        scratch_shapes=scratch,
        compiler_params=pltpu.CompilerParams(
            collective_id=0, has_side_effects=True, vmem_limit_bytes=63 * 1024 * 1024),
    )(x, step.T, decay.reshape(1, H), b, c, dy, q, k, v, o)
    return (res[0], res[1].T) + tuple(res[2:])


def solution(mesh):
    nc, nh = mesh.shape["ctx"], mesh.shape["head"]
    tok = P(("ctx", "head"), None)
    both = P("ctx", "head")
    return jax.shard_map(
        functools.partial(per_device, nc, nh),
        mesh=mesh,
        in_specs=(both, both, P("head"), both, both, both, tok, tok, tok, tok),
        out_specs=(both, both, both, both, tok, tok, tok),
        check_vma=False,
    )
```
